32 devices in a mesh: groups: 2 (over x), expert: 8 (over z, y), cuts: 2 (over core).
Axes of the slice: x: 2, y: 2, z: 4, core: 2. Of those that a mesh axis runs over, the one named last changes fastest.
Arguments:
- tokens: bfloat16 [512, 3584], P(('groups', 'expert', 'cuts')), parts along dimension 0, may hold values from -6 to 6
- expert_ids: int32 [512, 2], P(('groups', 'expert', 'cuts')), parts along dimension 0, may hold values from 0 to 1, as said below
- route_weights: float32 [512, 2], P(('groups', 'expert', 'cuts')), parts along dimension 0, may hold values from 0.2 to 1
- gate_weight: bfloat16 [3584, 6144], P(None, ('expert', 'cuts')), may hold values from -0.09375 to 0.09375
- up_weight: bfloat16 [3584, 6144], P(None, ('expert', 'cuts')), may hold values from -0.09375 to 0.09375
- down_weight: bfloat16 [3584, 6144], P(None, ('expert', 'cuts')), may hold values from -0.109375 to 0.109375
Outputs:
- moe_output: bfloat16 [512, 3584], P(('groups', 'expert', 'cuts')), parts along dimension 0
The draws below stay inside these ranges and needn't reach their ends.
There are 2 independent parts, one for each index of `groups`. The reference program is written for one: setup_inputs(seed, part) draws one part's arguments, and reference() takes and returns one part's arrays. A program takes and returns all parts, laid end to end along the dimension named above; an argument that names none is the same for every part. Nothing has to cross between parts.
Inputs may be any that keep to these rules, and one draw needn't show every extreme that they name: `expert_ids`: each row names two different experts. Within each device's aligned block of 16 rows no expert is named more than 16 times, and in every draw one expert is named exactly 16 times in every block.
All inputs are finite; a program needn't handle non-finite values.
Results may differ from the reference program's by a relative error of at most 0.0057.
Values may be sent and summed in bfloat16 or wider, within the bound.
A program may use at most 64 MiB of HBM per device.

```python
import jax
import jax.numpy as jnp
from jax import lax

D = 3584
FF = 3072
TOK_DEV = 16
EXPERTS = 2
CAP = 16
TOKENS = 256
N_EXPERT = 8
N_CUTS = 2


def draw_expert_ids(key, part):
    key = jax.random.fold_in(key, 3)
    block_count = N_EXPERT * N_CUTS
    hot_expert = jax.random.randint(jax.random.fold_in(key, 5), (), 0, EXPERTS)

    def one_block(block_key):
        perm_key, order_key, flip_key = jax.random.split(block_key, 3)
        others = (hot_expert + 1 + jnp.arange((EXPERTS - 1) * CAP, dtype=jnp.int32) // CAP) % EXPERTS
        chosen = jax.random.permutation(perm_key, others)[:2 * TOK_DEV - CAP]
        sequence = jnp.sort(jnp.concatenate([jnp.full((CAP,), hot_expert, jnp.int32), chosen.astype(jnp.int32)]))
        paired = jnp.stack([sequence[:TOK_DEV], sequence[TOK_DEV:]], axis=1)
        order = jax.random.permutation(order_key, TOK_DEV)
        paired = paired[order]
        flips = jax.random.randint(flip_key, (TOK_DEV,), 0, 2)
        paired = jnp.where(flips[:, None] == 1, paired[:, ::-1], paired)
        return paired.astype(jnp.int32)
    block_keys = jax.random.split(jax.random.fold_in(key, 7), block_count)
    ids_all = jax.vmap(one_block)(block_keys)
    return ids_all.reshape(TOKENS, 2)


def levels(stream_key, shape, pieces, least, high):
    level, own = 1.0, jax.random.fold_in(stream_key, 6)
    for axis_at, parts in pieces:
        steps = jnp.exp(jax.random.uniform(jax.random.fold_in(own, axis_at), (parts,), jnp.float32, least / len(pieces), high / len(pieces)))
        level = level * jnp.repeat(steps, shape[axis_at] // parts).reshape([-1 if axis == axis_at else 1 for axis in range(len(shape))])
    return level


def normal_values(own_key, shape, deviation, most, pieces=(), kind=jnp.bfloat16):
    drawn = deviation * jax.random.normal(own_key, shape, jnp.float32)
    if pieces:
        drawn = drawn * levels(own_key, shape, pieces, -0.22, 0.18)
    return jnp.clip(drawn, -most, most).astype(kind)


def setup_inputs(seed: int = 0, part: int = 0) -> dict:
    streams_of = jax.random.split(jax.random.key(seed), 7)
    part_keys = jax.random.split(jax.random.fold_in(streams_of[6], part), 7)
    tokens = normal_values(part_keys[0], (TOKENS, D), 1.0, 6.0, ((0, 16),))
    expert_ids = draw_expert_ids(jax.random.fold_in(jax.random.fold_in(streams_of[6], part), 71), part)
    route_weights = jnp.clip(0.2 + 0.8 * jax.random.uniform(part_keys[2], (TOKENS, 2), jnp.float32) ** levels(part_keys[2], (TOKENS, 2), ((0, 16),), -0.2, 0.2), 0.2, 1.0)
    gate_weight = normal_values(streams_of[3], (D, EXPERTS * FF), D ** -0.5, 0.09375, ((1, 16),))
    up_weight = normal_values(streams_of[4], (D, EXPERTS * FF), D ** -0.5, 0.09375, ((1, 16),))
    down_weight = normal_values(streams_of[5], (D, EXPERTS * FF), FF ** -0.5, 0.109375, ((1, 16),))
    return dict(tokens=tokens, expert_ids=expert_ids, route_weights=route_weights, gate_weight=gate_weight, up_weight=up_weight, down_weight=down_weight)


def expert_block(block_rows, w_gate, w_up, w_down):
    gate_proj = jnp.dot(block_rows, w_gate, preferred_element_type=jnp.float32)
    up_proj = jnp.dot(block_rows, w_up, preferred_element_type=jnp.float32)
    hidden = (jax.nn.silu(gate_proj) * up_proj).astype(jnp.bfloat16)
    return jnp.dot(hidden, w_down.T, preferred_element_type=jnp.float32).astype(jnp.bfloat16)


def slot_table(expert_ids):
    block_ids = expert_ids.reshape(-1, TOK_DEV * 2)
    onehot = (block_ids[:, :, None] == jnp.arange(EXPERTS, dtype=jnp.int32)[None, None, :]).astype(jnp.int32)
    earlier = jnp.cumsum(onehot, axis=1) - onehot
    return jnp.sum(earlier * onehot, axis=2).reshape(-1, 2).astype(jnp.int32)


def reference(tokens, expert_ids, route_weights, gate_weight, up_weight, down_weight):
    token_count = tokens.shape[0]
    slot_ids = slot_table(expert_ids)
    source_dev = jnp.arange(token_count, dtype=jnp.int32) // TOK_DEV
    positions = (source_dev[:, None] * CAP + slot_ids).astype(jnp.int32)
    slot_total = N_EXPERT * N_CUTS * CAP
    dispatch_buffer = jnp.zeros((EXPERTS, slot_total, D), tokens.dtype)
    spread_rows = jnp.broadcast_to(tokens[:, None, :], (token_count, 2, D))
    dispatch_buffer = dispatch_buffer.at[expert_ids, positions].set(spread_rows)

    def run_expert(expert_num):
        offset = (expert_num * FF).astype(jnp.int32)
        w_gate = lax.dynamic_slice_in_dim(gate_weight, offset, FF, 1)
        w_up = lax.dynamic_slice_in_dim(up_weight, offset, FF, 1)
        w_down = lax.dynamic_slice_in_dim(down_weight, offset, FF, 1)
        return expert_block(dispatch_buffer[expert_num], w_gate, w_up, w_down)

    outputs = lax.map(run_expert, jnp.arange(EXPERTS, dtype=jnp.int32))
    picked = outputs[expert_ids, positions].astype(jnp.float32)
    mixed_rows = jnp.sum(route_weights[:, :, None] * picked, axis=1)
    return mixed_rows.astype(jnp.bfloat16)
```

```python
import functools

import jax
import jax.numpy as jnp
from jax import lax
from jax.experimental import pallas as pl
from jax.experimental.pallas import tpu as pltpu
from jax.sharding import PartitionSpec as P

SPREAD = 4


def swapped(block, axis, distance):
    count = lax.axis_size(axis)
    route = []
    for low in range(count):
        high = low | 1 << distance
        if high != low and high < count:
            route += [(low, high), (high, low)]
    return lax.ppermute(block, axis, route)


def hidden_part(block_rows, w_gate, w_up):
    gate_proj = jnp.dot(block_rows, w_gate, preferred_element_type=jnp.float32)
    up_proj = jnp.dot(block_rows, w_up, preferred_element_type=jnp.float32)
    return (jax.nn.silu(gate_proj) * up_proj).astype(jnp.bfloat16)


def expert_part(block_rows, w_gate, w_up, w_down):
    hidden = hidden_part(block_rows, w_gate, w_up)
    return lax.dot_general(
        hidden, w_down, (((1,), (1,)), ((), ())), preferred_element_type=jnp.float32
    )


def per_device(tokens, expert_ids, route_weights, gate_weight, up_weight, down_weight):
    tok_rows, feat_width = tokens.shape
    n_expert = lax.axis_size("expert")
    experts = n_expert // SPREAD
    capacity = min(tok_rows, 2 * ((2 * tok_rows + experts - 1) // experts))
    quarter = feat_width // SPREAD
    my_index = lax.axis_index("expert")
    flat_ids = expert_ids.reshape(-1)
    onehot = (flat_ids[:, None] == jnp.arange(experts, dtype=jnp.int32)[None, :]).astype(jnp.int32)
    earlier = jnp.cumsum(onehot, axis=0) - onehot
    slot_ids = jnp.sum(earlier * onehot, axis=1).reshape(tok_rows, 2)
    targets = expert_ids * capacity + slot_ids
    columns = jnp.arange(experts * capacity, dtype=jnp.int32)
    placing = jnp.any(targets[None, :, :] == columns[:, None, None], axis=2).astype(jnp.bfloat16)
    outgoing = jnp.dot(placing, tokens, preferred_element_type=jnp.float32).astype(jnp.bfloat16)
    outgoing = outgoing.reshape(experts, capacity, feat_width)
    copies = jnp.repeat(outgoing, SPREAD, axis=0)
    arrived = lax.all_to_all(copies, "expert", split_axis=0, concat_axis=0, tiled=True)
    row_piece = lax.all_gather(arrived, "cuts", axis=0, tiled=True)
    piece_rows = row_piece.reshape(-1, feat_width)
    result_rows = expert_part(piece_rows, gate_weight, up_weight, down_weight)
    partial_terms = result_rows.reshape(row_piece.shape)
    partial_value = lax.psum_scatter(
        partial_terms, "cuts", scatter_dimension=0, tiled=True
    ).reshape(n_expert * capacity, feat_width)
    summed = partial_value
    for bit_level in (1, 0):
        half_width = summed.shape[1] // 2
        upper_half = my_index >> bit_level & 1 == 1
        lower_part = summed[:, :half_width]
        upper_part = summed[:, half_width:]
        kept_part = jnp.where(upper_half, upper_part, lower_part)
        given_part = jnp.where(upper_half, lower_part, upper_part)
        summed = kept_part + swapped(given_part, "expert", bit_level)
    expert_rows = summed.astype(jnp.bfloat16).reshape(n_expert, capacity, quarter)
    returned = lax.all_to_all(expert_rows, "expert", split_axis=0, concat_axis=0, tiled=True)
    results = returned.reshape(experts, SPREAD, capacity, quarter).transpose(0, 2, 1, 3)
    results = results.reshape(experts * capacity, feat_width)
    weighting = jnp.sum(
        jnp.where(targets[:, :, None] == columns[None, None, :], route_weights[:, :, None], 0.0),
        axis=1,
    )
    mixed_rows = jnp.dot(
        weighting,
        results.astype(jnp.float32),
        precision=lax.Precision.HIGHEST,
        preferred_element_type=jnp.float32,
    )
    return mixed_rows.astype(jnp.bfloat16)


CHOICES = 2
LANES = 128
CORE_LAG, PAIR_LAG, LINE_LAG = 1, 3, 5


def chunk_width(feat_width):
    for width in (512, 256, 128):
        if feat_width % width == 0:
            return width
    return feat_width


def dense_kernel(
    experts, tok, ids, mix, w_gate, w_up, w_down, out,
    gate_v, up_v, down_v, rows, scale, gate_acc, up_acc,
    kept_core, core_out, core_in, kept_pair, pair_out, pair_in, kept_line, line_out, line_in,
    w_sem, own_sem, g_send, g_recv, s_send, s_recv, r_send, r_recv,
):
    chunks, _, _, line, height, width = rows.shape
    n_expert = lax.axis_size("expert")
    place, core = lax.axis_index("expert"), lax.axis_index("cuts")
    along, side = place // 2, place % 2
    core_peer = {"cuts": 1 - core}
    pair_peer = {"expert": along * 2 + 1 - side}
    line_peers = [{"expert": lax.rem(along + step, line) * 2 + side} for step in range(1, line)]
    peers = [core_peer, pair_peer] + line_peers
    my_expert = place // (n_expert // experts)

    loads = [
        pltpu.make_async_copy(source, target, w_sem.at[at])
        for at, (source, target) in enumerate(((w_gate, gate_v), (w_up, up_v), (w_down, down_v)))
    ]
    own = [
        pltpu.make_async_copy(tok.at[:, pl.ds(j * width, width)], rows.at[j, 0, 0, 0], own_sem.at[j])
        for j in range(chunks)
    ]
    for copy in own + loads:
        copy.start()
    lane = lax.broadcasted_iota(jnp.int32, (height, LANES), 1)
    own_scale = jnp.zeros((height, LANES), jnp.float32)
    for k in range(CHOICES):
        own_scale += jnp.where(lane == ids[:, k:k + 1], mix[:, k:k + 1], 0.0)
    scale[0, 0, 0] = own_scale

    barrier = pltpu.get_barrier_semaphore()
    for peer in peers:
        pl.semaphore_signal(barrier, inc=1, device_id=peer, device_id_type=pl.DeviceIdType.MESH)
    pl.semaphore_wait(barrier, len(peers))

    def send(source, target, send_sem, recv_sem, peer):
        copy = pltpu.make_async_remote_copy(
            src_ref=source, dst_ref=target, send_sem=send_sem, recv_sem=recv_sem,
            device_id=peer, device_id_type=pl.DeviceIdType.MESH,
        )
        copy.start()
        return copy

    sent = {}
    for j in range(chunks):
        mine = tok.at[:, pl.ds(j * width, width)]
        for step in range(1, line):
            sent[j, step] = send(
                mine, rows.at[j, 0, 0, line - step], g_send.at[j, step], g_recv.at[j, line - step],
                line_peers[step - 1],
            )
        sent[j, "pair own"] = send(
            mine, rows.at[j, 0, 1, 0], g_send.at[j, line], g_recv.at[j, line], pair_peer
        )
    for step in range(1, line):
        sent["s", step] = send(
            scale.at[0, 0, 0], scale.at[0, 0, line - step], s_send.at[step], s_recv.at[line - step],
            line_peers[step - 1],
        )

    for turn in range(chunks + 2):
        if turn < chunks:
            j = turn
            for step in range(1, line):
                sent[j, line - step].wait_recv()
            sent[j, "pair"] = send(
                rows.at[j, 0, 0, pl.ds(1, line - 1)], rows.at[j, 0, 1, pl.ds(1, line - 1)],
                g_send.at[j, line + 1], g_recv.at[j, line + 1], pair_peer,
            )
            own[j].wait()
            sent[j, "core"] = send(
                rows.at[j, 0, 0], rows.at[j, 1, 0],
                g_send.at[j, line + 2], g_recv.at[j, line + 2], core_peer,
            )
        if turn == chunks - 1:
            for step in range(1, line):
                sent["s", line - step].wait_recv()
            sent["s", "pair"] = send(
                scale.at[0, 0], scale.at[0, 1], s_send.at[line], s_recv.at[line], pair_peer
            )
        if 1 <= turn <= chunks:
            j = turn - 1
            sent[j, "pair own"].wait_recv()
            sent[j, "pair"].wait_recv()
            sent[j, "core pair"] = send(
                rows.at[j, 0, 1], rows.at[j, 1, 1],
                g_send.at[j, line + 3], g_recv.at[j, line + 3], core_peer,
            )
        if turn == chunks:
            sent["s", "pair"].wait_recv()
            sent["s", "core"] = send(
                scale.at[0], scale.at[1], s_send.at[line + 1], s_recv.at[line + 1], core_peer
            )
        if turn >= 2:
            j = turn - 2
            sent[j, "core"].wait_recv()
            sent[j, "core pair"].wait_recv()
            if j == 0:
                loads[0].wait()
                loads[1].wait()
            block = rows[j].reshape(-1, width)
            depth = pl.ds(j * width, width)
            gate_part = jnp.dot(block, gate_v[depth, :], preferred_element_type=jnp.float32)
            up_part = jnp.dot(block, up_v[depth, :], preferred_element_type=jnp.float32)
            if j == 0:
                gate_acc[...] = gate_part
                up_acc[...] = up_part
            else:
                gate_acc[...] += gate_part
                up_acc[...] += up_part

    gate = gate_acc[...]
    hidden = (gate / (1.0 + jnp.exp(-gate)) * up_acc[...]).astype(jnp.bfloat16)
    sent["s", "core"].wait_recv()
    weights = scale[...].reshape(-1, LANES)
    lane = lax.broadcasted_iota(jnp.int32, weights.shape, 1)
    weight = jnp.sum(jnp.where(lane == my_expert, weights, 0.0), axis=1, keepdims=True)
    loads[2].wait()

    pair_rows, line_rows = 2 * line * height, line * height
    back = {}
    for turn in range(chunks + LINE_LAG):
        if turn < chunks:
            j = turn
            part = weight * lax.dot_general(
                hidden, down_v[pl.ds(j * width, width), :], (((1,), (1,)), ((), ())),
                preferred_element_type=jnp.float32,
            )
            core_out[j] = part[pair_rows:].astype(jnp.bfloat16)
            back[j, "core"] = send(
                core_out.at[j], core_in.at[j], r_send.at[j, 0], r_recv.at[j, 0], core_peer
            )
            kept_core[j] = part[:pair_rows]
        if 0 <= turn - CORE_LAG < chunks:
            j = turn - CORE_LAG
            back[j, "core"].wait_recv()
            part = kept_core[j, line_rows:] + core_in[j, line_rows:].astype(jnp.float32)
            pair_out[j] = part.astype(jnp.bfloat16)
            back[j, "pair"] = send(
                pair_out.at[j], pair_in.at[j], r_send.at[j, line], r_recv.at[j, line], pair_peer
            )
            kept_pair[j] = kept_core[j, :line_rows] + core_in[j, :line_rows].astype(jnp.float32)
        if 0 <= turn - PAIR_LAG < chunks:
            j = turn - PAIR_LAG
            back[j, "pair"].wait_recv()
            part = kept_pair[j] + pair_in[j].astype(jnp.float32)
            line_out[j] = part[height:].astype(jnp.bfloat16).reshape(line - 1, height, width)
            for step in range(1, line):
                back[j, step] = send(
                    line_out.at[j, step - 1], line_in.at[j, step - 1],
                    r_send.at[j, step], r_recv.at[j, step], line_peers[step - 1],
                )
            kept_line[j] = part[:height]
        if 0 <= turn - LINE_LAG < chunks:
            j = turn - LINE_LAG
            total = kept_line[j]
            for step in range(1, line):
                back[j, step].wait_recv()
                total += line_in[j, step - 1].astype(jnp.float32)
            out[:, pl.ds(j * width, width)] = total.astype(out.dtype)
    for copy in list(sent.values()) + list(back.values()):
        copy.wait_send()


def dense_device(tokens, expert_ids, route_weights, gate_weight, up_weight, down_weight):
    height, feat_width = tokens.shape
    units = gate_weight.shape[1]
    n_expert = lax.axis_size("expert")
    experts = n_expert // SPREAD
    line = n_expert // 2
    width = chunk_width(feat_width)
    chunks = feat_width // width
    total = 4 * line * height
    bf16, f32 = jnp.bfloat16, jnp.float32
    dma = pltpu.SemaphoreType.DMA
    vmem, anywhere = pl.BlockSpec(memory_space=pltpu.VMEM), pl.BlockSpec(memory_space=pl.ANY)
    return pl.pallas_call(
        functools.partial(dense_kernel, experts),
        out_shape=jax.ShapeDtypeStruct((height, feat_width), bf16),
        in_specs=[anywhere, vmem, vmem, anywhere, anywhere, anywhere],
        out_specs=vmem,
        scratch_shapes=[
            pltpu.VMEM((feat_width, units), bf16),
            pltpu.VMEM((feat_width, units), bf16),
            pltpu.VMEM((feat_width, units), bf16),
            pltpu.VMEM((chunks, 2, 2, line, height, width), bf16),
            pltpu.VMEM((2, 2, line, height, LANES), f32),
            pltpu.VMEM((total, units), f32),
            pltpu.VMEM((total, units), f32),
            pltpu.VMEM((chunks, total // 2, width), f32),
            pltpu.VMEM((chunks, total // 2, width), bf16),
            pltpu.VMEM((chunks, total // 2, width), bf16),
            pltpu.VMEM((chunks, total // 4, width), f32),
            pltpu.VMEM((chunks, total // 4, width), bf16),
            pltpu.VMEM((chunks, total // 4, width), bf16),
            pltpu.VMEM((chunks, height, width), f32),
            pltpu.VMEM((chunks, line - 1, height, width), bf16),
            pltpu.VMEM((chunks, line - 1, height, width), bf16),
            dma((3,)),
            dma((chunks,)),
            dma((chunks, line + 4)),
            dma((chunks, line + 4)),
            dma((line + 2,)),
            dma((line + 2,)),
            dma((chunks, line + 1)),
            dma((chunks, line + 1)),
        ],
        compiler_params=pltpu.CompilerParams(
            collective_id=0, has_side_effects=True, vmem_limit_bytes=40 * 1024 * 1024
        ),
        cost_estimate=pl.CostEstimate(
            flops=6 * total * feat_width * units,
            bytes_accessed=6 * feat_width * units,
            transcendentals=total * units,
        ),
    )(tokens, expert_ids, route_weights, gate_weight, up_weight, down_weight)


def solution(mesh):
    in_specs = (
        P(("groups", "expert", "cuts"), None),
        P(("groups", "expert", "cuts"), None),
        P(("groups", "expert", "cuts"), None),
        P(None, ("expert", "cuts")),
        P(None, ("expert", "cuts")),
        P(None, ("expert", "cuts")),
    )
    out_specs = P(("groups", "expert", "cuts"), None)
    dense = mesh.shape["expert"] == CHOICES * SPREAD and mesh.shape["cuts"] == 2
    return jax.shard_map(
        dense_device if dense else per_device, mesh=mesh, in_specs=in_specs, out_specs=out_specs, check_vma=False
    )
```

```python
import functools

import jax
import jax.numpy as jnp
from jax import lax
from jax.experimental import pallas as pl
from jax.experimental.pallas import tpu as pltpu
from jax.sharding import PartitionSpec as P

SPREAD = 4


def swapped(block, axis, distance):
    count = lax.axis_size(axis)
    route = []
    for low in range(count):
        high = low | 1 << distance
        if high != low and high < count:
            route += [(low, high), (high, low)]
    return lax.ppermute(block, axis, route)


def hidden_part(block_rows, w_gate, w_up):
    gate_proj = jnp.dot(block_rows, w_gate, preferred_element_type=jnp.float32)
    up_proj = jnp.dot(block_rows, w_up, preferred_element_type=jnp.float32)
    return (jax.nn.silu(gate_proj) * up_proj).astype(jnp.bfloat16)


def expert_part(block_rows, w_gate, w_up, w_down):
    hidden = hidden_part(block_rows, w_gate, w_up)
    return lax.dot_general(
        hidden, w_down, (((1,), (1,)), ((), ())), preferred_element_type=jnp.float32
    )


def per_device(tokens, expert_ids, route_weights, gate_weight, up_weight, down_weight):
    tok_rows, feat_width = tokens.shape
    n_expert = lax.axis_size("expert")
    experts = n_expert // SPREAD
    capacity = min(tok_rows, 2 * ((2 * tok_rows + experts - 1) // experts))
    quarter = feat_width // SPREAD
    my_index = lax.axis_index("expert")
    flat_ids = expert_ids.reshape(-1)
    onehot = (flat_ids[:, None] == jnp.arange(experts, dtype=jnp.int32)[None, :]).astype(jnp.int32)
    earlier = jnp.cumsum(onehot, axis=0) - onehot
    slot_ids = jnp.sum(earlier * onehot, axis=1).reshape(tok_rows, 2)
    targets = expert_ids * capacity + slot_ids
    columns = jnp.arange(experts * capacity, dtype=jnp.int32)
    placing = jnp.any(targets[None, :, :] == columns[:, None, None], axis=2).astype(jnp.bfloat16)
    outgoing = jnp.dot(placing, tokens, preferred_element_type=jnp.float32).astype(jnp.bfloat16)
    outgoing = outgoing.reshape(experts, capacity, feat_width)
    copies = jnp.repeat(outgoing, SPREAD, axis=0)
    arrived = lax.all_to_all(copies, "expert", split_axis=0, concat_axis=0, tiled=True)
    row_piece = lax.all_gather(arrived, "cuts", axis=0, tiled=True)
    piece_rows = row_piece.reshape(-1, feat_width)
    result_rows = expert_part(piece_rows, gate_weight, up_weight, down_weight)
    partial_terms = result_rows.reshape(row_piece.shape)
    partial_value = lax.psum_scatter(
        partial_terms, "cuts", scatter_dimension=0, tiled=True
    ).reshape(n_expert * capacity, feat_width)
    summed = partial_value
    for bit_level in (1, 0):
        half_width = summed.shape[1] // 2
        upper_half = my_index >> bit_level & 1 == 1
        lower_part = summed[:, :half_width]
        upper_part = summed[:, half_width:]
        kept_part = jnp.where(upper_half, upper_part, lower_part)
        given_part = jnp.where(upper_half, lower_part, upper_part)
        summed = kept_part + swapped(given_part, "expert", bit_level)
    expert_rows = summed.astype(jnp.bfloat16).reshape(n_expert, capacity, quarter)
    returned = lax.all_to_all(expert_rows, "expert", split_axis=0, concat_axis=0, tiled=True)
    results = returned.reshape(experts, SPREAD, capacity, quarter).transpose(0, 2, 1, 3)
    results = results.reshape(experts * capacity, feat_width)
    weighting = jnp.sum(
        jnp.where(targets[:, :, None] == columns[None, None, :], route_weights[:, :, None], 0.0),
        axis=1,
    )
    mixed_rows = jnp.dot(
        weighting,
        results.astype(jnp.float32),
        precision=lax.Precision.HIGHEST,
        preferred_element_type=jnp.float32,
    )
    return mixed_rows.astype(jnp.bfloat16)


CHOICES = 2
LANES = 128
CORE_LAG, PAIR_LAG, LINE_LAG = 1, 4, 7
GATHER_WIDTHS, SCATTER_WIDTHS = (1792, 512, 256, 128), (512, 256, 128)


def chunk_width(feat_width, widths):
    for width in widths:
        if feat_width % width == 0:
            return width
    return feat_width


def dense_kernel(
    experts, tok, ids, mix, w_gate, w_up, w_down, out,
    ids_v, mix_v, gate_v, up_v, down_v, rows, scale, gate_acc, up_acc,
    kept_core, core_out, core_in, kept_pair, pair_out, pair_in, kept_line, line_out, line_in,
    w_sem, own_sem, up_send, down_send, line_recv, pair_send, pair_recv, core_send, core_recv, s_send, s_recv, r_send, r_recv,
):
    chunks, _, _, line, height, width = rows.shape
    n_expert = lax.axis_size("expert")
    place, core = lax.axis_index("expert"), lax.axis_index("cuts")
    along, side = place // 2, place % 2
    up_peer = {"expert": lax.rem(along + 1, line) * 2 + side}
    down_peer = {"expert": lax.rem(along + line - 1, line) * 2 + side}
    core_peer = {"cuts": 1 - core}
    pair_peer = {"expert": along * 2 + 1 - side}
    line_peers = [{"expert": lax.rem(along + step, line) * 2 + side} for step in range(1, line)]
    peers = [core_peer, pair_peer] + line_peers
    my_expert = place // (n_expert // experts)

    loads = [
        pltpu.make_async_copy(source, target, w_sem.at[at])
        for at, (source, target) in enumerate(((w_gate, gate_v), (w_up, up_v), (w_down, down_v)))
    ]
    own = [
        pltpu.make_async_copy(tok.at[:, pl.ds(j * width, width)], rows.at[j, 0, 0, 0], own_sem.at[j])
        for j in range(chunks)
    ]
    small = [
        pltpu.make_async_copy(ids, ids_v, w_sem.at[3]),
        pltpu.make_async_copy(mix, mix_v, w_sem.at[4]),
    ]
    for copy in small + own + loads:
        copy.start()
    barrier = pltpu.get_barrier_semaphore()
    for peer in peers:
        pl.semaphore_signal(barrier, inc=1, device_id=peer, device_id_type=pl.DeviceIdType.MESH)
    pl.semaphore_wait(barrier, len(peers))

    def send(source, target, send_sem, recv_sem, peer):
        copy = pltpu.make_async_remote_copy(
            src_ref=source, dst_ref=target, send_sem=send_sem, recv_sem=recv_sem,
            device_id=peer, device_id_type=pl.DeviceIdType.MESH,
        )
        copy.start()
        return copy

    def mine(j):
        return tok.at[:, pl.ds(j * width, width)]

    def to_line(j, step, upward):
        held = line - step if upward else step
        slot = line - step - 1 if upward else step + 1
        return pltpu.make_async_remote_copy(
            src_ref=mine(j) if step == 0 else rows.at[j, 0, 0, held],
            dst_ref=rows.at[j, 0, 0, slot],
            send_sem=(up_send if upward else down_send).at[j, step],
            recv_sem=line_recv.at[j, slot],
            device_id=up_peer if upward else down_peer,
            device_id_type=pl.DeviceIdType.MESH,
        )

    def holds(step, upward):
        return along >= step if upward else along <= line - 1 - step

    def passes(step, upward):
        return holds(step, upward) & (along < line - 1 if upward else along > 0)

    def to_pair(j, slot):
        return pltpu.make_async_remote_copy(
            src_ref=mine(j) if slot == 0 else rows.at[j, 0, 0, slot],
            dst_ref=rows.at[j, 0, 1, slot],
            send_sem=pair_send.at[j, slot], recv_sem=pair_recv.at[j, slot],
            device_id=pair_peer, device_id_type=pl.DeviceIdType.MESH,
        )

    def to_core(j, row, slot):
        return pltpu.make_async_remote_copy(
            src_ref=mine(j) if (row, slot) == (0, 0) else rows.at[j, 0, row, slot],
            dst_ref=rows.at[j, 1, row, slot],
            send_sem=core_send.at[j, row, slot], recv_sem=core_recv.at[j, row, slot],
            device_id=core_peer, device_id_type=pl.DeviceIdType.MESH,
        )

    for j in range(chunks):
        for upward in (True, False):
            pl.when(passes(0, upward))(lambda j=j, upward=upward: to_line(j, 0, upward).start())
        to_pair(j, 0).start()
    for j in range(chunks):
        to_core(j, 0, 0).start()
    for copy in small:
        copy.wait()
    diagonal = lax.broadcasted_iota(jnp.int32, (height, height), 0) == lax.broadcasted_iota(
        jnp.int32, (height, height), 1
    )
    lane = lax.broadcasted_iota(jnp.int32, (height, LANES), 1)
    own_scale = jnp.zeros((height, LANES), jnp.float32)
    for k in range(CHOICES):
        name = jnp.sum(jnp.where(diagonal, ids_v[k:k + 1, :], 0), axis=1, keepdims=True)
        share = jnp.sum(jnp.where(diagonal, mix_v[k:k + 1, :], 0.0), axis=1, keepdims=True)
        own_scale += jnp.where(lane == name, share, 0.0)
    scale[0, 0, 0] = own_scale
    sent = {}
    for step in range(1, line):
        sent["s", step] = send(
            scale.at[0, 0, 0], scale.at[0, 0, line - step], s_send.at[step], s_recv.at[line - step],
            line_peers[step - 1],
        )

    def line_arrival(j, step, upward):
        slot = line - step if upward else step
        to_line(j, step - 1, upward).wait_recv()
        if step < line - 1:
            pl.when(passes(step, upward))(lambda: to_line(j, step, upward).start())
        to_pair(j, slot).start()
        to_core(j, 0, slot).start()

    def pair_arrival(j, slot):
        to_pair(j, slot).wait_recv()
        to_core(j, 1, slot).start()

    for step in range(1, line + 1):
        for j in range(chunks):
            if step < line:
                for upward in (True, False):
                    pl.when(holds(step, upward))(
                        lambda j=j, step=step, upward=upward: line_arrival(j, step, upward)
                    )
            if step == 1:
                pair_arrival(j, 0)
            else:
                for upward in (True, False):
                    slot = line - step + 1 if upward else step - 1
                    pl.when(holds(step - 1, upward))(lambda j=j, slot=slot: pair_arrival(j, slot))
        if step == line - 2:
            for hop in range(1, line):
                sent["s", line - hop].wait_recv()
            sent["s", "pair"] = send(
                scale.at[0, 0], scale.at[0, 1], s_send.at[line], s_recv.at[line], pair_peer
            )
        if step == line - 1:
            sent["s", "pair"].wait_recv()
            sent["s", "core"] = send(
                scale.at[0], scale.at[1], s_send.at[line + 1], s_recv.at[line + 1], core_peer
            )
    loads[0].wait()
    loads[1].wait()
    for j in range(chunks):
        own[j].wait()
        for row in range(2):
            for slot in range(line):
                to_core(j, row, slot).wait_recv()
        block = rows[j].reshape(-1, width)
        depth = pl.ds(j * width, width)
        gate_part = jnp.dot(block, gate_v[depth, :], preferred_element_type=jnp.float32)
        up_part = jnp.dot(block, up_v[depth, :], preferred_element_type=jnp.float32)
        if j == 0:
            gate_acc[...] = gate_part
            up_acc[...] = up_part
        else:
            gate_acc[...] += gate_part
            up_acc[...] += up_part

    gate = gate_acc[...]
    hidden = (gate / (1.0 + jnp.exp(-gate)) * up_acc[...]).astype(jnp.bfloat16)
    sent["s", "core"].wait_recv()
    weights = scale[...].reshape(-1, LANES)
    lane = lax.broadcasted_iota(jnp.int32, weights.shape, 1)
    weight = jnp.sum(jnp.where(lane == my_expert, weights, 0.0), axis=1, keepdims=True)
    loads[2].wait()

    parts, _, span = core_out.shape
    pair_rows, line_rows = 2 * line * height, line * height
    back = {}
    for turn in range(parts + LINE_LAG):
        if turn < parts:
            j = turn
            part = weight * lax.dot_general(
                hidden, down_v[pl.ds(j * span, span), :], (((1,), (1,)), ((), ())),
                preferred_element_type=jnp.float32,
            )
            core_out[j] = part[pair_rows:].astype(jnp.bfloat16)
            back[j, "core"] = send(
                core_out.at[j], core_in.at[j], r_send.at[j, 0], r_recv.at[j, 0], core_peer
            )
            kept_core[j] = part[:pair_rows]
        if 0 <= turn - CORE_LAG < parts:
            j = turn - CORE_LAG
            back[j, "core"].wait_recv()
            part = kept_core[j, line_rows:] + core_in[j, line_rows:].astype(jnp.float32)
            pair_out[j] = part.astype(jnp.bfloat16)
            back[j, "pair"] = send(
                pair_out.at[j], pair_in.at[j], r_send.at[j, line], r_recv.at[j, line], pair_peer
            )
            kept_pair[j] = kept_core[j, :line_rows] + core_in[j, :line_rows].astype(jnp.float32)
        if 0 <= turn - PAIR_LAG < parts:
            j = turn - PAIR_LAG
            back[j, "pair"].wait_recv()
            part = kept_pair[j] + pair_in[j].astype(jnp.float32)
            line_out[j] = part[height:].astype(jnp.bfloat16).reshape(line - 1, height, span)
            for step in range(1, line):
                back[j, step] = send(
                    line_out.at[j, step - 1], line_in.at[j, step - 1],
                    r_send.at[j, step], r_recv.at[j, step], line_peers[step - 1],
                )
            kept_line[j] = part[:height]
        if 0 <= turn - LINE_LAG < parts:
            j = turn - LINE_LAG
            total = kept_line[j]
            for step in range(1, line):
                back[j, step].wait_recv()
                total += line_in[j, step - 1].astype(jnp.float32)
            out[:, pl.ds(j * span, span)] = total.astype(out.dtype)
    for j in range(chunks):
        for step in range(line - 1):
            for upward in (True, False):
                pl.when(passes(step, upward))(
                    lambda j=j, step=step, upward=upward: to_line(j, step, upward).wait_send()
                )
        for slot in range(line):
            to_pair(j, slot).wait_send()
            for row in range(2):
                to_core(j, row, slot).wait_send()
    for copy in list(sent.values()) + list(back.values()):
        copy.wait_send()


def dense_device(tokens, expert_ids, route_weights, gate_weight, up_weight, down_weight):
    height, feat_width = tokens.shape
    units = gate_weight.shape[1]
    n_expert = lax.axis_size("expert")
    experts = n_expert // SPREAD
    line = n_expert // 2
    width, span = chunk_width(feat_width, GATHER_WIDTHS), chunk_width(feat_width, SCATTER_WIDTHS)
    chunks, parts = feat_width // width, feat_width // span
    total = 4 * line * height
    bf16, f32 = jnp.bfloat16, jnp.float32
    dma = pltpu.SemaphoreType.DMA
    vmem, hbm = pl.BlockSpec(memory_space=pltpu.VMEM), pl.BlockSpec(memory_space=pltpu.HBM)
    return pl.pallas_call(
        functools.partial(dense_kernel, experts),
        out_shape=jax.ShapeDtypeStruct((height, feat_width), bf16),
        in_specs=[hbm] * 6,
        out_specs=vmem,
        scratch_shapes=[
            pltpu.VMEM((CHOICES, height), jnp.int32),
            pltpu.VMEM((CHOICES, height), f32),
            pltpu.VMEM((feat_width, units), bf16),
            pltpu.VMEM((feat_width, units), bf16),
            pltpu.VMEM((feat_width, units), bf16),
            pltpu.VMEM((chunks, 2, 2, line, height, width), bf16),
            pltpu.VMEM((2, 2, line, height, LANES), f32),
            pltpu.VMEM((total, units), f32),
            pltpu.VMEM((total, units), f32),
            pltpu.VMEM((parts, total // 2, span), f32),
            pltpu.VMEM((parts, total // 2, span), bf16),
            pltpu.VMEM((parts, total // 2, span), bf16),
            pltpu.VMEM((parts, total // 4, span), f32),
            pltpu.VMEM((parts, total // 4, span), bf16),
            pltpu.VMEM((parts, total // 4, span), bf16),
            pltpu.VMEM((parts, height, span), f32),
            pltpu.VMEM((parts, line - 1, height, span), bf16),
            pltpu.VMEM((parts, line - 1, height, span), bf16),
            dma((5,)),
            dma((chunks,)),
            dma((chunks, line)),
            dma((chunks, line)),
            dma((chunks, line)),
            dma((chunks, line)),
            dma((chunks, line)),
            dma((chunks, 2, line)),
            dma((chunks, 2, line)),
            dma((line + 2,)),
            dma((line + 2,)),
            dma((parts, line + 1)),
            dma((parts, line + 1)),
        ],
        compiler_params=pltpu.CompilerParams(
            collective_id=0, has_side_effects=True, vmem_limit_bytes=64000000
        ),
        cost_estimate=pl.CostEstimate(
            flops=6 * total * feat_width * units,
            bytes_accessed=6 * feat_width * units,
            transcendentals=total * units,
        ),
    )(tokens, expert_ids.T, route_weights.T, gate_weight, up_weight, down_weight)


def solution(mesh):
    in_specs = (
        P(("groups", "expert", "cuts"), None),
        P(("groups", "expert", "cuts"), None),
        P(("groups", "expert", "cuts"), None),
        P(None, ("expert", "cuts")),
        P(None, ("expert", "cuts")),
        P(None, ("expert", "cuts")),
    )
    out_specs = P(("groups", "expert", "cuts"), None)
    dense = mesh.shape["expert"] == CHOICES * SPREAD and mesh.shape["cuts"] == 2
    return jax.shard_map(
        dense_device if dense else per_device, mesh=mesh, in_specs=in_specs, out_specs=out_specs, check_vma=False
    )
```

```python
import functools

import jax
import jax.numpy as jnp
from jax import lax
from jax.experimental import pallas as pl
from jax.experimental.pallas import tpu as pltpu
from jax.sharding import PartitionSpec as P

SPREAD = 4


def swapped(block, axis, distance):
    count = lax.axis_size(axis)
    route = []
    for low in range(count):
        high = low | 1 << distance
        if high != low and high < count:
            route += [(low, high), (high, low)]
    return lax.ppermute(block, axis, route)


def hidden_part(block_rows, w_gate, w_up):
    gate_proj = jnp.dot(block_rows, w_gate, preferred_element_type=jnp.float32)
    up_proj = jnp.dot(block_rows, w_up, preferred_element_type=jnp.float32)
    return (jax.nn.silu(gate_proj) * up_proj).astype(jnp.bfloat16)


def expert_part(block_rows, w_gate, w_up, w_down):
    hidden = hidden_part(block_rows, w_gate, w_up)
    return lax.dot_general(
        hidden, w_down, (((1,), (1,)), ((), ())), preferred_element_type=jnp.float32
    )


def per_device(tokens, expert_ids, route_weights, gate_weight, up_weight, down_weight):
    tok_rows, feat_width = tokens.shape
    n_expert = lax.axis_size("expert")
    experts = n_expert // SPREAD
    capacity = min(tok_rows, 2 * ((2 * tok_rows + experts - 1) // experts))
    quarter = feat_width // SPREAD
    my_index = lax.axis_index("expert")
    flat_ids = expert_ids.reshape(-1)
    onehot = (flat_ids[:, None] == jnp.arange(experts, dtype=jnp.int32)[None, :]).astype(jnp.int32)
    earlier = jnp.cumsum(onehot, axis=0) - onehot
    slot_ids = jnp.sum(earlier * onehot, axis=1).reshape(tok_rows, 2)
    targets = expert_ids * capacity + slot_ids
    columns = jnp.arange(experts * capacity, dtype=jnp.int32)
    placing = jnp.any(targets[None, :, :] == columns[:, None, None], axis=2).astype(jnp.bfloat16)
    outgoing = jnp.dot(placing, tokens, preferred_element_type=jnp.float32).astype(jnp.bfloat16)
    outgoing = outgoing.reshape(experts, capacity, feat_width)
    copies = jnp.repeat(outgoing, SPREAD, axis=0)
    arrived = lax.all_to_all(copies, "expert", split_axis=0, concat_axis=0, tiled=True)
    row_piece = lax.all_gather(arrived, "cuts", axis=0, tiled=True)
    piece_rows = row_piece.reshape(-1, feat_width)
    result_rows = expert_part(piece_rows, gate_weight, up_weight, down_weight)
    partial_terms = result_rows.reshape(row_piece.shape)
    partial_value = lax.psum_scatter(
        partial_terms, "cuts", scatter_dimension=0, tiled=True
    ).reshape(n_expert * capacity, feat_width)
    summed = partial_value
    for bit_level in (1, 0):
        half_width = summed.shape[1] // 2
        upper_half = my_index >> bit_level & 1 == 1
        lower_part = summed[:, :half_width]
        upper_part = summed[:, half_width:]
        kept_part = jnp.where(upper_half, upper_part, lower_part)
        given_part = jnp.where(upper_half, lower_part, upper_part)
        summed = kept_part + swapped(given_part, "expert", bit_level)
    expert_rows = summed.astype(jnp.bfloat16).reshape(n_expert, capacity, quarter)
    returned = lax.all_to_all(expert_rows, "expert", split_axis=0, concat_axis=0, tiled=True)
    results = returned.reshape(experts, SPREAD, capacity, quarter).transpose(0, 2, 1, 3)
    results = results.reshape(experts * capacity, feat_width)
    weighting = jnp.sum(
        jnp.where(targets[:, :, None] == columns[None, None, :], route_weights[:, :, None], 0.0),
        axis=1,
    )
    mixed_rows = jnp.dot(
        weighting,
        results.astype(jnp.float32),
        precision=lax.Precision.HIGHEST,
        preferred_element_type=jnp.float32,
    )
    return mixed_rows.astype(jnp.bfloat16)


CHOICES = 2
LANES = 128
CORE_LAG, PAIR_LAG, LINE_LAG = 1, 4, 7
GATHER_LAG = 2
GATHER_WIDTHS, SCATTER_WIDTHS = (1792, 512, 256, 128), (512, 256, 128)


def chunk_width(feat_width, widths):
    for width in widths:
        if feat_width % width == 0:
            return width
    return feat_width


def dense_kernel(
    experts, tok, ids, mix, w_gate, w_up, w_down, out,
    ids_v, mix_v, gate_v, up_v, down_v, rows, scale, gate_acc, up_acc,
    kept_core, core_out, core_in, kept_pair, pair_out, pair_in, kept_line, line_out, line_in,
    w_sem, own_sem, up_send, down_send, line_recv, pair_send, pair_recv, core_send, core_recv, s_send, s_recv, r_send, r_recv, mixed, out_sem,
):
    chunks, _, _, line, height, width = rows.shape
    n_expert = lax.axis_size("expert")
    place, core = lax.axis_index("expert"), lax.axis_index("cuts")
    along, side = place // 2, place % 2
    up_peer = {"expert": lax.rem(along + 1, line) * 2 + side}
    down_peer = {"expert": lax.rem(along + line - 1, line) * 2 + side}
    core_peer = {"cuts": 1 - core}
    pair_peer = {"expert": along * 2 + 1 - side}
    line_peers = [{"expert": lax.rem(along + step, line) * 2 + side} for step in range(1, line)]
    peers = [core_peer, pair_peer] + line_peers
    my_expert = place // (n_expert // experts)

    loads = [
        pltpu.make_async_copy(source, target, w_sem.at[at])
        for at, (source, target) in enumerate(((w_gate, gate_v), (w_up, up_v), (w_down, down_v)))
    ]
    own = [
        pltpu.make_async_copy(tok.at[:, pl.ds(j * width, width)], rows.at[j, 0, 0, 0], own_sem.at[j])
        for j in range(chunks)
    ]
    small = [
        pltpu.make_async_copy(ids, ids_v, w_sem.at[3]),
        pltpu.make_async_copy(mix, mix_v, w_sem.at[4]),
    ]
    for copy in small + own + loads:
        copy.start()
    barrier = pltpu.get_barrier_semaphore()
    for peer in peers:
        pl.semaphore_signal(barrier, inc=1, device_id=peer, device_id_type=pl.DeviceIdType.MESH)
    pl.semaphore_wait(barrier, len(peers))

    def send(source, target, send_sem, recv_sem, peer):
        copy = pltpu.make_async_remote_copy(
            src_ref=source, dst_ref=target, send_sem=send_sem, recv_sem=recv_sem,
            device_id=peer, device_id_type=pl.DeviceIdType.MESH,
        )
        copy.start()
        return copy

    def mine(j):
        return tok.at[:, pl.ds(j * width, width)]

    def to_line(j, step, upward):
        held = line - step if upward else step
        slot = line - step - 1 if upward else step + 1
        return pltpu.make_async_remote_copy(
            src_ref=mine(j) if step == 0 else rows.at[j, 0, 0, held],
            dst_ref=rows.at[j, 0, 0, slot],
            send_sem=(up_send if upward else down_send).at[j, step],
            recv_sem=line_recv.at[j, slot],
            device_id=up_peer if upward else down_peer,
            device_id_type=pl.DeviceIdType.MESH,
        )

    def holds(step, upward):
        return along >= step if upward else along <= line - 1 - step

    def passes(step, upward):
        return holds(step, upward) & (along < line - 1 if upward else along > 0)

    def to_pair(j, slot):
        return pltpu.make_async_remote_copy(
            src_ref=mine(j) if slot == 0 else rows.at[j, 0, 0, slot],
            dst_ref=rows.at[j, 0, 1, slot],
            send_sem=pair_send.at[j, slot], recv_sem=pair_recv.at[j, slot],
            device_id=pair_peer, device_id_type=pl.DeviceIdType.MESH,
        )

    def to_core(j, row, slot):
        return pltpu.make_async_remote_copy(
            src_ref=mine(j) if (row, slot) == (0, 0) else rows.at[j, 0, row, slot],
            dst_ref=rows.at[j, 1, row, slot],
            send_sem=core_send.at[j, row, slot], recv_sem=core_recv.at[j, row, slot],
            device_id=core_peer, device_id_type=pl.DeviceIdType.MESH,
        )

    for j in range(chunks):
        for upward in (True, False):
            pl.when(passes(0, upward))(lambda j=j, upward=upward: to_line(j, 0, upward).start())
        to_pair(j, 0).start()
    for j in range(chunks):
        to_core(j, 0, 0).start()
    for copy in small:
        copy.wait()
    diagonal = lax.broadcasted_iota(jnp.int32, (height, height), 0) == lax.broadcasted_iota(
        jnp.int32, (height, height), 1
    )
    lane = lax.broadcasted_iota(jnp.int32, (height, LANES), 1)
    own_scale = jnp.zeros((height, LANES), jnp.float32)
    for k in range(CHOICES):
        name = jnp.sum(jnp.where(diagonal, ids_v[k:k + 1, :], 0), axis=1, keepdims=True)
        share = jnp.sum(jnp.where(diagonal, mix_v[k:k + 1, :], 0.0), axis=1, keepdims=True)
        own_scale += jnp.where(lane == name, share, 0.0)
    scale[0, 0, 0] = own_scale
    sent = {}
    for step in range(1, line):
        sent["s", step] = send(
            scale.at[0, 0, 0], scale.at[0, 0, line - step], s_send.at[step], s_recv.at[line - step],
            line_peers[step - 1],
        )

    def line_arrival(j, step, upward):
        slot = line - step if upward else step
        to_line(j, step - 1, upward).wait_recv()
        if step < line - 1:
            pl.when(passes(step, upward))(lambda: to_line(j, step, upward).start())
        to_pair(j, slot).start()
        to_core(j, 0, slot).start()

    def pair_arrival(j, slot):
        to_pair(j, slot).wait_recv()
        to_core(j, 1, slot).start()

    for turn in range(1, line + GATHER_LAG):
        if turn < line:
            for j in range(chunks):
                for upward in (True, False):
                    pl.when(holds(turn, upward))(
                        lambda j=j, step=turn, upward=upward: line_arrival(j, step, upward)
                    )
        step = turn - GATHER_LAG
        for j in range(chunks):
            if step == 0:
                pair_arrival(j, 0)
            elif step > 0:
                for upward in (True, False):
                    slot = line - step if upward else step
                    pl.when(holds(step, upward))(lambda j=j, slot=slot: pair_arrival(j, slot))
        if turn == line - 1:
            for hop in range(1, line):
                sent["s", line - hop].wait_recv()
            sent["s", "pair"] = send(
                scale.at[0, 0], scale.at[0, 1], s_send.at[line], s_recv.at[line], pair_peer
            )
        if turn == line:
            sent["s", "pair"].wait_recv()
            sent["s", "core"] = send(
                scale.at[0], scale.at[1], s_send.at[line + 1], s_recv.at[line + 1], core_peer
            )
    loads[0].wait()
    loads[1].wait()
    for j in range(chunks):
        own[j].wait()
        for row in range(2):
            for slot in range(line):
                to_core(j, row, slot).wait_recv()
        block = rows[j].reshape(-1, width)
        depth = pl.ds(j * width, width)
        gate_part = jnp.dot(block, gate_v[depth, :], preferred_element_type=jnp.float32)
        up_part = jnp.dot(block, up_v[depth, :], preferred_element_type=jnp.float32)
        if j == 0:
            gate_acc[...] = gate_part
            up_acc[...] = up_part
        else:
            gate_acc[...] += gate_part
            up_acc[...] += up_part

    gate = gate_acc[...]
    hidden = (gate / (1.0 + jnp.exp(-gate)) * up_acc[...]).astype(jnp.bfloat16)
    sent["s", "core"].wait_recv()
    weights = scale[...].reshape(-1, LANES)
    lane = lax.broadcasted_iota(jnp.int32, weights.shape, 1)
    weight = jnp.sum(jnp.where(lane == my_expert, weights, 0.0), axis=1, keepdims=True)
    loads[2].wait()

    parts, _, span = core_out.shape
    pair_rows, line_rows = 2 * line * height, line * height
    back = {}
    for turn in range(parts + LINE_LAG):
        if turn < parts:
            j = turn
            part = weight * lax.dot_general(
                hidden, down_v[pl.ds(j * span, span), :], (((1,), (1,)), ((), ())),
                preferred_element_type=jnp.float32,
            )
            core_out[j] = part[pair_rows:].astype(jnp.bfloat16)
            back[j, "core"] = send(
                core_out.at[j], core_in.at[j], r_send.at[j, 0], r_recv.at[j, 0], core_peer
            )
            kept_core[j] = part[:pair_rows]
        if 0 <= turn - CORE_LAG < parts:
            j = turn - CORE_LAG
            back[j, "core"].wait_recv()
            part = kept_core[j, line_rows:] + core_in[j, line_rows:].astype(jnp.float32)
            pair_out[j] = part.astype(jnp.bfloat16)
            back[j, "pair"] = send(
                pair_out.at[j], pair_in.at[j], r_send.at[j, line], r_recv.at[j, line], pair_peer
            )
            kept_pair[j] = kept_core[j, :line_rows] + core_in[j, :line_rows].astype(jnp.float32)
        if 0 <= turn - PAIR_LAG < parts:
            j = turn - PAIR_LAG
            back[j, "pair"].wait_recv()
            part = kept_pair[j] + pair_in[j].astype(jnp.float32)
            line_out[j] = part[height:].astype(jnp.bfloat16).reshape(line - 1, height, span)
            for step in range(1, line):
                back[j, step] = send(
                    line_out.at[j, step - 1], line_in.at[j, step - 1],
                    r_send.at[j, step], r_recv.at[j, step], line_peers[step - 1],
                )
            kept_line[j] = part[:height]
        if 0 <= turn - LINE_LAG < parts:
            j = turn - LINE_LAG
            total = kept_line[j]
            for step in range(1, line):
                back[j, step].wait_recv()
                total += line_in[j, step - 1].astype(jnp.float32)
            mixed[j] = total.astype(mixed.dtype)
            back[j, "out"] = pltpu.make_async_copy(
                mixed.at[j], out.at[:, pl.ds(j * span, span)], out_sem.at[j]
            )
            back[j, "out"].start()
    for j in range(chunks):
        for step in range(line - 1):
            for upward in (True, False):
                pl.when(passes(step, upward))(
                    lambda j=j, step=step, upward=upward: to_line(j, step, upward).wait_send()
                )
        for slot in range(line):
            to_pair(j, slot).wait_send()
            for row in range(2):
                to_core(j, row, slot).wait_send()
    for key, copy in list(sent.items()) + list(back.items()):
        if key[1] == "out":
            copy.wait()
        else:
            copy.wait_send()


def dense_device(tokens, expert_ids, route_weights, gate_weight, up_weight, down_weight):
    height, feat_width = tokens.shape
    units = gate_weight.shape[1]
    n_expert = lax.axis_size("expert")
    experts = n_expert // SPREAD
    line = n_expert // 2
    width, span = chunk_width(feat_width, GATHER_WIDTHS), chunk_width(feat_width, SCATTER_WIDTHS)
    chunks, parts = feat_width // width, feat_width // span
    total = 4 * line * height
    bf16, f32 = jnp.bfloat16, jnp.float32
    dma = pltpu.SemaphoreType.DMA
    hbm = pl.BlockSpec(memory_space=pltpu.HBM)
    return pl.pallas_call(
        functools.partial(dense_kernel, experts),
        out_shape=jax.ShapeDtypeStruct((height, feat_width), bf16),
        in_specs=[hbm] * 6,
        out_specs=hbm,
        scratch_shapes=[
            pltpu.VMEM((CHOICES, height), jnp.int32),
            pltpu.VMEM((CHOICES, height), f32),
            pltpu.VMEM((feat_width, units), bf16),
            pltpu.VMEM((feat_width, units), bf16),
            pltpu.VMEM((feat_width, units), bf16),
            pltpu.VMEM((chunks, 2, 2, line, height, width), bf16),
            pltpu.VMEM((2, 2, line, height, LANES), f32),
            pltpu.VMEM((total, units), f32),
            pltpu.VMEM((total, units), f32),
            pltpu.VMEM((parts, total // 2, span), f32),
            pltpu.VMEM((parts, total // 2, span), bf16),
            pltpu.VMEM((parts, total // 2, span), bf16),
            pltpu.VMEM((parts, total // 4, span), f32),
            pltpu.VMEM((parts, total // 4, span), bf16),
            pltpu.VMEM((parts, total // 4, span), bf16),
            pltpu.VMEM((parts, height, span), f32),
            pltpu.VMEM((parts, line - 1, height, span), bf16),
            pltpu.VMEM((parts, line - 1, height, span), bf16),
            dma((5,)),
            dma((chunks,)),
            dma((chunks, line)),
            dma((chunks, line)),
            dma((chunks, line)),
            dma((chunks, line)),
            dma((chunks, line)),
            dma((chunks, 2, line)),
            dma((chunks, 2, line)),
            dma((line + 2,)),
            dma((line + 2,)),
            dma((parts, line + 1)),
            dma((parts, line + 1)),
            pltpu.VMEM((parts, height, span), bf16),
            dma((parts,)),
        ],
        compiler_params=pltpu.CompilerParams(
            collective_id=0, has_side_effects=True, vmem_limit_bytes=64000000
        ),
        cost_estimate=pl.CostEstimate(
            flops=6 * total * feat_width * units,
            bytes_accessed=6 * feat_width * units,
            transcendentals=total * units,
        ),
    )(tokens, expert_ids.T, route_weights.T, gate_weight, up_weight, down_weight)


def solution(mesh):
    in_specs = (
        P(("groups", "expert", "cuts"), None),
        P(("groups", "expert", "cuts"), None),
        P(("groups", "expert", "cuts"), None),
        P(None, ("expert", "cuts")),
        P(None, ("expert", "cuts")),
        P(None, ("expert", "cuts")),
    )
    out_specs = P(("groups", "expert", "cuts"), None)
    dense = mesh.shape["expert"] == CHOICES * SPREAD and mesh.shape["cuts"] == 2
    return jax.shard_map(
        dense_device if dense else per_device, mesh=mesh, in_specs=in_specs, out_specs=out_specs, check_vma=False
    )
```
